32 devices in a mesh: region: 8 (over z, core), layer: 4 (over y, x).
Axes of the slice: x: 2, y: 2, z: 4, core: 2. Of those that a mesh axis runs over, the one named last changes fastest.
Arguments:
- right_side: float32 [64, 131072], P(None, ('region', 'layer')), may hold values from -72 to 72
- block_entries: float32 [2048, 7, 4096], P(('region', 'layer')), may hold values from -0.01875 to 2.01875, as said below
- neighbours: int32 [2048, 6], P(('region', 'layer')), may hold values from 0 to 95
- face_rows: int32 [128, 8], P(('region', 'layer')), may hold values from 0 to 63
- die_owner: int32 [16384, 1], P(('region', 'layer')), may hold values from 0 to 3; in each aligned block of 512 rows (0 to 511, 512 to 1023, ...) at most 128 rows name the same one
- die_node: int32 [16384], P(('region', 'layer')), may hold values from 0 to 4095
Outputs:
- solution_field: float32 [64, 131072], P(None, ('region', 'layer'))
- residual: float32 [64, 131072], P(None, ('region', 'layer'))
- mech_temps: float32 [128, 8192], P(('region', 'layer'))
The draws below stay inside these ranges and needn't reach their ends.
Inputs may be any that keep to these rules, and one draw needn't show every extreme that they name: `block_entries`: dense blocks of the conduction operator: the diagonal block of each block row carries the node's own coupling on its diagonal. `die_owner`: among the 512 rows of one device, at most 128 name the same owner, and in some devices exactly 128 do.
All inputs are finite; a program needn't handle non-finite values.
Results may differ from the reference program's by a relative error of at most 0.0003.
Values sent between devices are 32-bit elements; how exact they have to be, the bound alone decides.
A program may use at most 128 MiB of HBM per device.

```python
import math
import jax
import jax.numpy as jnp
import numpy as np
from jax import lax

BLOCK = 64
RHS = 64
COUPLED = 7
BLK_DEV = 64
DIE_ROWS = 512
SLOTS = 128
FACES = 8
BLOCKS_ALL = 2048
NODES = 131072
N_REGION = 8
N_LAYER = 4


def draw_block_entries(key, part):
    first_key, second_key = jax.random.split(key)
    spread = 1.2 / BLOCK
    shape_all = (BLOCKS_ALL, COUPLED, BLOCK * BLOCK)
    entries = jax.random.uniform(first_key, shape_all, jnp.float32, -spread, spread)
    diag_vals = jax.random.uniform(second_key, (BLOCKS_ALL, 1, BLOCK), jnp.float32, 1.0, 2.0)
    spread_diag = jnp.repeat(diag_vals, BLOCK, axis=2)
    position = jnp.arange(BLOCK * BLOCK)
    on_diag = (position // BLOCK == position % BLOCK)[None, :] & (jnp.arange(COUPLED)[:, None] == 0)
    return entries + jnp.where(on_diag[None, :, :], spread_diag, jnp.float32(0.0))


def draw_right_side(key, part):
    keys = jax.random.split(key, 3)
    node_scale = jnp.exp(jax.random.uniform(keys[0], (1, NODES), jnp.float32, math.log(0.3), math.log(3.0)))
    column_scale = jnp.exp(jax.random.uniform(keys[1], (RHS, 1), jnp.float32, math.log(0.5), math.log(2.0)))
    ramp = 1.0 + 2.0 * jnp.arange(NODES, dtype=jnp.float32)[None, :] / jnp.float32(NODES - 1)
    base = jnp.clip(jax.random.normal(keys[2], (RHS, NODES), jnp.float32), -4.0, 4.0)
    return base * node_scale * ramp * column_scale


def place_ends(result, key, low, high):
    longest = result.shape.index(max(result.shape))
    spots = []
    for shift in (0, 1):
        where = [jax.random.randint(jax.random.fold_in(key, axis), (), 0, length) for axis, length in enumerate(result.shape)]
        where[longest] = (where[longest] + shift) % result.shape[longest]
        spots.append(tuple(where))
    return result.at[spots[0]].set(low).at[spots[1]].set(high)


def deal_out(stream_key, own, number, rows, amount, top, reach, lean):
    sequence = jax.random.permutation(stream_key, amount)
    packed, usual = load_shares(amount, rows * top, reach, lean, True), load_shares(amount, rows * top, reach, lean, False)
    places = jnp.arange(amount)

    def named(lengths, offset_by):
        used = int((lengths > 0).sum())
        fixed = max(1, used // 4)
        shifted = fixed + (places - fixed + offset_by * (used - fixed)) % max(1, amount - fixed)
        return jnp.zeros((amount,), jnp.int32).at[sequence[jnp.where(places < fixed, places, shifted)]].set(jnp.asarray(lengths, jnp.int32))

    lengths = jnp.where(number % 4 == 0, named(packed, number // 4), named(usual, number - number // 4 - 1))
    mixed = jax.random.permutation(jax.random.fold_in(own, 3), amount)
    giver, sink = mixed[0:amount // 2 * 2:2], mixed[1:amount // 2 * 2:2]
    room = jnp.minimum(lengths[giver] - 1, reach - lengths[sink]) // 2
    room = jnp.where((giver == sequence[0]) | (sink == sequence[0]) | (lengths[sink] == 0), 0, jnp.maximum(room, 0))
    shifted = jax.random.randint(jax.random.fold_in(own, 4), (amount // 2,), 0, 1 << 20) % (room + 1)
    lengths = lengths.at[giver].add(-shifted).at[sink].add(shifted)
    labels = jnp.searchsorted(jnp.cumsum(lengths), jnp.arange(rows * top), side="right").astype(jnp.int32)
    table = labels.reshape(top, rows).T
    table = table[jax.random.permutation(jax.random.fold_in(own, 1), rows)]
    offset_by = jax.random.randint(jax.random.fold_in(own, 2), (rows, 1), 0, top)
    return jnp.take_along_axis(table, (jnp.arange(top)[None, :] + offset_by) % top, axis=1)


def load_shares(amount, total, most, slope, full):
    portions = [(1 << 20) // math.isqrt(rank ** slope) + 1 for rank in range(1, amount + 1)]
    largest = most if full else min(most, max(-(-total // amount), total * portions[0] // sum(portions)))
    least = 1 if total - largest >= amount - 1 else 0
    given, rest = [largest] + [least] * (amount - 1), total - largest - least * (amount - 1)
    while rest > 0:
        movable = [i for i in range(1, amount) if given[i] < largest] or [i for i in range(1, amount) if given[i] < most]
        mass, left = sum([portions[i] for i in movable]), rest
        for i in movable:
            addition = min(most - given[i], max(1, left * portions[i] // mass), rest)
            given[i] = given[i] + addition
            rest = rest - addition
    return np.array(given)


def setup_inputs(seed: int = 0) -> dict:
    key_of = jax.random.split(jax.random.key(seed), 7)
    right_side = draw_right_side(jax.random.fold_in(key_of[6], 71), 0)
    block_entries = draw_block_entries(jax.random.fold_in(key_of[6], 71), 0)
    neighbours = place_ends(jax.random.randint(key_of[2], (BLOCKS_ALL, COUPLED - 1), 0, BLK_DEV + 4 * FACES), jax.random.fold_in(key_of[2], 1), 0, (BLK_DEV + 4 * FACES) - 1).astype(jnp.int32)
    face_rows = place_ends(jax.random.randint(key_of[3], (N_REGION * N_LAYER * 4, FACES), 0, BLK_DEV), jax.random.fold_in(key_of[3], 1), 0, BLK_DEV - 1).astype(jnp.int32)
    die_owner_keys = jax.random.split(jax.random.fold_in(key_of[4], 1), (N_REGION * N_LAYER * DIE_ROWS) // DIE_ROWS)
    die_owner_turns = jax.random.permutation(jax.random.fold_in(key_of[4], 3), (N_REGION * N_LAYER * DIE_ROWS) // DIE_ROWS)
    die_owner = jax.vmap(lambda own, number: deal_out(jax.random.fold_in(key_of[4], 2), own, number, DIE_ROWS, N_LAYER, 1, SLOTS, 2))(die_owner_keys, die_owner_turns).reshape((N_REGION * N_LAYER * DIE_ROWS, 1))
    die_node = place_ends(jax.random.randint(key_of[5], (N_REGION * N_LAYER * DIE_ROWS,), 0, BLK_DEV * BLOCK), jax.random.fold_in(key_of[5], 1), 0, (BLK_DEV * BLOCK) - 1).astype(jnp.int32)
    return dict(right_side=right_side, block_entries=block_entries, neighbours=neighbours, face_rows=face_rows, die_owner=die_owner, die_node=die_node)


def exact_dot(left, right):
    return jnp.dot(left.astype(jnp.float32), right.astype(jnp.float32), precision=lax.Precision.HIGHEST, preferred_element_type=jnp.float32)

def chol_solve(matrix, target):
    lower_factor = jnp.linalg.cholesky(matrix)
    halfway = lax.linalg.triangular_solve(lower_factor, target, left_side=True, lower=True)
    return lax.linalg.triangular_solve(lower_factor, halfway, left_side=True, lower=True, transpose_a=True)

def place_rows(values_rows, owners):
    owner_hits = (owners[:, None] == jnp.arange(N_LAYER, dtype=jnp.int32)[None, :]).astype(jnp.int32)
    earlier_hits = jnp.cumsum(owner_hits, axis=0, dtype=jnp.int32) - owner_hits
    rank_index = jnp.sum(earlier_hits * owner_hits, axis=1, dtype=jnp.int32)
    slot_index = owners * SLOTS + rank_index
    empty_rows = jnp.zeros((N_LAYER * SLOTS, values_rows.shape[1]), values_rows.dtype)
    return empty_rows.at[slot_index].set(values_rows)

def peer_tables():
    device_count = N_REGION * N_LAYER
    device_ids = np.arange(device_count)
    region_ids = device_ids // N_LAYER
    layer_ids = device_ids % N_LAYER
    near_idx = (region_ids ^ 1) * N_LAYER + layer_ids
    far_idx = (region_ids ^ N_REGION // 2) * N_LAYER + layer_ids
    below_idx = region_ids * N_LAYER + np.maximum(layer_ids - 1, 0)
    above_idx = region_ids * N_LAYER + np.minimum(layer_ids + 1, N_LAYER - 1)
    has_below = (layer_ids > 0).astype(np.float32)
    has_above = (layer_ids < N_LAYER - 1).astype(np.float32)
    return (jnp.asarray(near_idx, dtype=jnp.int32), jnp.asarray(far_idx, dtype=jnp.int32), jnp.asarray(below_idx, dtype=jnp.int32), jnp.asarray(above_idx, dtype=jnp.int32), jnp.asarray(has_below, dtype=jnp.float32), jnp.asarray(has_above, dtype=jnp.float32))

def apply_all(field, block_entries, neighbours, face_rows):
    device_count = N_REGION * N_LAYER
    near_idx, far_idx, below_idx, above_idx, has_below, has_above = peer_tables()
    tiles = field.reshape(RHS, device_count, BLK_DEV, BLOCK).transpose(1, 0, 2, 3)
    face_list = face_rows.reshape(device_count, 4 * FACES)

    def pick_faces(tile_set, chosen):
        return jnp.take(tile_set, chosen, axis=1)
    outgoing = jax.vmap(pick_faces)(tiles, face_list).reshape(device_count, RHS, 4, FACES, BLOCK)
    near_rows = outgoing[near_idx, :, 0]
    far_rows = outgoing[far_idx, :, 1]
    below_rows = outgoing[below_idx, :, 2] * has_below[:, None, None, None]
    above_rows = outgoing[above_idx, :, 3] * has_above[:, None, None, None]
    tile_mats = block_entries.reshape(device_count, BLK_DEV, COUPLED, BLOCK, BLOCK)
    neighbour_sets = neighbours.reshape(device_count, BLK_DEV * (COUPLED - 1))

    def device_product(inputs):
        own_tiles, near_part, far_part, below_part, above_part, mats_here, chosen = inputs
        extended = jnp.concatenate([own_tiles, near_part, far_part, below_part, above_part], axis=1)
        picked = jnp.take(extended, chosen, axis=1).reshape(RHS, BLK_DEV, COUPLED - 1, BLOCK)
        columns = jnp.concatenate([own_tiles[:, :, None, :], picked], axis=2)
        return jnp.einsum('snkb,nkab->sna', columns, mats_here, precision=lax.Precision.HIGHEST)
    product = lax.map(device_product, (tiles, near_rows, far_rows, below_rows, above_rows, tile_mats, neighbour_sets))
    return product.transpose(1, 0, 2, 3).reshape(RHS, device_count * BLK_DEV * BLOCK)

def reference(right_side, block_entries, neighbours, face_rows, die_owner, die_node):
    device_count = N_REGION * N_LAYER
    resid_zero = right_side
    norm_zero = exact_dot(resid_zero, resid_zero.T)
    image_zero = apply_all(resid_zero, block_entries, neighbours, face_rows)
    curve_zero = exact_dot(resid_zero, image_zero.T)
    alpha_first = chol_solve(0.5 * (curve_zero + curve_zero.T), norm_zero)
    iterate_one = exact_dot(alpha_first.T, resid_zero)
    resid_one = resid_zero - exact_dot(alpha_first.T, image_zero)
    norm_one = exact_dot(resid_one, resid_one.T)
    beta_step = chol_solve(norm_zero, norm_one)
    direction = resid_one + exact_dot(beta_step.T, resid_zero)
    image_one = apply_all(direction, block_entries, neighbours, face_rows)
    curve_one = exact_dot(direction, image_one.T)
    alpha_second = chol_solve(0.5 * (curve_one + curve_one.T), norm_one)
    solution_field = iterate_one + exact_dot(alpha_second.T, direction)
    residual = resid_one - exact_dot(alpha_second.T, image_one)
    by_device = solution_field.reshape(RHS, device_count, BLK_DEV * BLOCK).transpose(1, 2, 0)

    def pick_rows(local_field, chosen):
        return jnp.take(local_field, chosen, axis=0)
    die_rows = jax.vmap(pick_rows)(by_device, die_node.reshape(device_count, DIE_ROWS))
    buffers = jax.vmap(place_rows)(die_rows, die_owner.reshape(device_count, DIE_ROWS))
    buffers = buffers.reshape(N_REGION, N_LAYER, N_LAYER, SLOTS * RHS).transpose(0, 2, 1, 3)
    mech_temps = buffers.reshape(N_REGION * N_LAYER * N_LAYER, SLOTS * RHS)
    return (solution_field, residual, mech_temps)
```

```python
import functools

import jax
import jax.numpy as jnp
from jax import lax
from jax.experimental import pallas as pl
from jax.experimental.pallas import tpu as pltpu
from jax.sharding import PartitionSpec as P

BLOCK = 64
RHS = 64
COUPLED = 7
BLK_DEV = 64
SLOTS = 128
FACES = 8
GROUP = 8
MESH = pl.DeviceIdType.MESH
F32 = jnp.float32
BF16 = jnp.bfloat16
VMEM = functools.partial(pl.BlockSpec, memory_space=pltpu.VMEM)
SMEM = functools.partial(pl.BlockSpec, memory_space=pltpu.SMEM)
BIG = 48 * 1024 * 1024


def dot_hi(left, right, dims=((1,), (0,))):
    return lax.dot_general(
        left, right, (dims, ((), ())), precision=lax.Precision.HIGHEST, preferred_element_type=F32
    )


def exchange_kernel(regions, layers, faces_ref, field_ref, out_ref, send_buf, send_sem, recv_sem):
    region = lax.axis_index("region")
    layer = lax.axis_index("layer")
    near = region + 1 - 2 * lax.rem(region, 2)
    far = lax.rem(region + regions // 2, regions)
    peers = (
        (near, layer),
        (far, layer),
        (region, lax.max(layer - 1, 0)),
        (region, lax.min(layer + 1, layers - 1)),
    )
    has = (None, None, layer > 0, layer < layers - 1)
    landing = (0, 1, 3, 2)

    def guarded(m, action):
        if has[m] is None:
            action()
        else:
            pl.when(has[m])(action)

    barrier = pltpu.get_barrier_semaphore()
    for m in range(4):

        def greet(m=m):
            pl.semaphore_signal(barrier, inc=1, device_id=peers[m], device_id_type=MESH)

        guarded(m, greet)
    for m in range(4):
        for j in range(FACES // 2):
            first = field_ref[faces_ref[m * FACES + 2 * j]]
            second = field_ref[faces_ref[m * FACES + 2 * j + 1]]
            send_buf[m, j] = jnp.concatenate([first, second], axis=1)
    pl.semaphore_wait(barrier, 2 + lax.min(layer, 1) + lax.min(layers - 1 - layer, 1))

    def copy_of(m):
        return pltpu.make_async_remote_copy(
            src_ref=send_buf.at[SENDS[m]],
            dst_ref=out_ref.at[landing[m]],
            send_sem=send_sem.at[m],
            recv_sem=recv_sem.at[landing[m]],
            device_id=peers[m],
            device_id_type=MESH,
        )

    for m in range(4):
        guarded(m, lambda m=m: copy_of(m).start())
    for m in (2, 3):

        def blank(m=m):
            out_ref[m] = jnp.zeros_like(out_ref[m])

        pl.when(jnp.logical_not(has[m]))(blank)
    for m in range(4):
        guarded(m, lambda m=m: copy_of(m).wait_send())
    for m in range(4):

        def arrive(m=m):
            pltpu.make_async_remote_copy(
                src_ref=send_buf.at[m],
                dst_ref=out_ref.at[m],
                send_sem=send_sem.at[m],
                recv_sem=recv_sem.at[m],
                device_id=peers[m],
                device_id_type=MESH,
            ).wait_recv()

        guarded(m, arrive)


SENDS = (0, 1, 3, 2)


def exchange(faces, field, regions, layers, number):
    return pl.pallas_call(
        functools.partial(exchange_kernel, regions, layers),
        out_shape=jax.ShapeDtypeStruct((4, FACES // 2, BLOCK, 2 * RHS), F32),
        in_specs=[SMEM(), VMEM()],
        out_specs=VMEM(),
        scratch_shapes=[
            pltpu.VMEM((4, FACES // 2, BLOCK, 2 * RHS), F32),
            pltpu.SemaphoreType.DMA((4,)),
            pltpu.SemaphoreType.DMA((4,)),
        ],
        compiler_params=pltpu.CompilerParams(
            collective_id=number, has_side_effects=True, vmem_limit_bytes=BIG
        ),
        name="face_exchange",
    )(faces, field)


def split_pair(block):
    upper = block.astype(BF16)
    return upper, (block - upper.astype(F32)).astype(BF16)


def load_extended(field_ref, recv_ref, ext):
    @pl.loop(0, BLK_DEV, unroll=4)
    def _(n):
        upper, lower = split_pair(field_ref[n])
        ext[n] = jnp.concatenate([upper, lower], axis=1)

    for m in range(4):
        for j in range(FACES // 2):
            pair = recv_ref[m, j]
            for half in range(2):
                upper, lower = split_pair(pair[:, half * RHS : (half + 1) * RHS])
                ext[BLK_DEV + m * FACES + 2 * j + half] = jnp.concatenate([upper, lower], axis=1)


def product_of(left, neigh_ref, ext, i):
    parts = [ext[i]]
    for k in range(COUPLED - 1):
        parts.append(ext[neigh_ref[i * (COUPLED - 1) + k]])
    full = jnp.dot(left, jnp.concatenate(parts, axis=0), preferred_element_type=F32)
    rows = full[:BLOCK] + full[BLOCK:]
    return rows[:, :RHS] + rows[:, RHS:]


def first_kernel(neigh_ref, mats_ref, field_ref, recv_ref, out_ref, left_ref, ext, spread):
    group = pl.program_id(0)

    @pl.when(group == 0)
    def _():
        load_extended(field_ref, recv_ref, ext)

    for k in range(COUPLED):
        for c in range(BLOCK // 2):
            spread[k, pl.ds(c * GROUP, GROUP), :] = mats_ref[k, :, c * 128 : (c + 1) * 128]
    low = lax.broadcasted_iota(jnp.int32, (BLOCK // 2, 128), 1) < BLOCK
    for sub in range(GROUP):
        i = group * GROUP + sub
        tiles = [spread[k, pl.ds(sub, BLOCK // 2, stride=GROUP), :] for k in range(COUPLED)]
        turned = [pltpu.roll(tile, BLOCK, 1) for tile in tiles]
        uppers, lowers = [], []
        for k in range(0, COUPLED, 2):
            if k + 1 < COUPLED:
                even = jnp.where(low, tiles[k], turned[k + 1])
                odd = jnp.where(low, turned[k], tiles[k + 1])
            else:
                even, odd = tiles[k][:, :BLOCK], turned[k][:, :BLOCK]
            upper, lower = split_pair(jnp.concatenate([even, odd], axis=0))
            uppers.append(upper)
            lowers.append(lower)
        left = jnp.concatenate(
            [jnp.concatenate(uppers, axis=1), jnp.concatenate(lowers, axis=1)], axis=0
        )
        left_ref[sub] = left
        rows = product_of(left, neigh_ref, ext, i)
        for odd in range(2):
            out_ref[pl.ds(sub * BLOCK + odd, BLOCK // 2, stride=2), :] = rows[
                odd * BLOCK // 2 : (odd + 1) * BLOCK // 2
            ]


def second_kernel(neigh_ref, left_ref, field_ref, recv_ref, base_ref, near_ref, out_ref, gram_ref, ext):
    group = pl.program_id(0)

    @pl.when(group == 0)
    def _():
        load_extended(field_ref, recv_ref, ext)
        gram_ref[...] = jnp.zeros_like(gram_ref)

    for sub in range(GROUP):
        i = group * GROUP + sub
        rows = product_of(left_ref[sub], neigh_ref, ext, i)
        for odd in range(2):
            out_ref[pl.ds(sub * BLOCK + odd, BLOCK // 2, stride=2), :] = rows[
                odd * BLOCK // 2 : (odd + 1) * BLOCK // 2
            ]
    pair = jnp.concatenate([base_ref[...], near_ref[...]], axis=1)
    own = dot_hi(pair, pair, ((0,), (0,)))
    cross = dot_hi(pair, out_ref[...], ((0,), (0,)))
    gram_ref[0:64] += own[:64]
    gram_ref[64:128] += jnp.concatenate([own[64:, 64:], cross[:64]], axis=1)
    gram_ref[128:192] += jnp.concatenate([cross[64:], cross[64:]], axis=1)


def apply_first(neigh, mats, field, recv):
    rows = GROUP * BLOCK
    grid = BLK_DEV // GROUP
    return pl.pallas_call(
        first_kernel,
        grid=(grid,),
        out_shape=[
            jax.ShapeDtypeStruct((BLK_DEV * BLOCK, RHS), F32),
            jax.ShapeDtypeStruct((BLK_DEV, 2 * BLOCK, COUPLED * BLOCK), BF16),
        ],
        in_specs=[
            SMEM(),
            pl.BlockSpec((COUPLED, GROUP, BLOCK * BLOCK), lambda g: (0, g, 0)),
            pl.BlockSpec((BLK_DEV, BLOCK, RHS), lambda g: (0, 0, 0)),
            pl.BlockSpec((4, FACES // 2, BLOCK, 2 * RHS), lambda g: (0, 0, 0, 0)),
        ],
        out_specs=[
            pl.BlockSpec((rows, RHS), lambda g: (g, 0)),
            pl.BlockSpec((GROUP, 2 * BLOCK, COUPLED * BLOCK), lambda g: (g, 0, 0)),
        ],
        scratch_shapes=[
            pltpu.VMEM((BLK_DEV + 4 * FACES, BLOCK, 2 * RHS), BF16),
            pltpu.VMEM((COUPLED, GROUP * BLOCK // 2, 128), F32),
        ],
        compiler_params=pltpu.CompilerParams(vmem_limit_bytes=BIG),
        name="operator_first",
    )(neigh, mats, field, recv)


def apply_second(neigh, lefts, field, recv, base):
    rows = GROUP * BLOCK
    grid = BLK_DEV // GROUP
    return pl.pallas_call(
        second_kernel,
        grid=(grid,),
        out_shape=[
            jax.ShapeDtypeStruct((BLK_DEV * BLOCK, RHS), F32),
            jax.ShapeDtypeStruct((192, 128), F32),
        ],
        in_specs=[
            SMEM(),
            pl.BlockSpec((GROUP, 2 * BLOCK, COUPLED * BLOCK), lambda g: (g, 0, 0)),
            pl.BlockSpec((BLK_DEV, BLOCK, RHS), lambda g: (0, 0, 0)),
            pl.BlockSpec((4, FACES // 2, BLOCK, 2 * RHS), lambda g: (0, 0, 0, 0)),
            pl.BlockSpec((rows, RHS), lambda g: (g, 0)),
            pl.BlockSpec((rows, RHS), lambda g: (g, 0)),
        ],
        out_specs=[
            pl.BlockSpec((rows, RHS), lambda g: (g, 0)),
            pl.BlockSpec((192, 128), lambda g: (0, 0)),
        ],
        scratch_shapes=[pltpu.VMEM((BLK_DEV + 4 * FACES, BLOCK, 2 * RHS), BF16)],
        compiler_params=pltpu.CompilerParams(vmem_limit_bytes=BIG),
        name="operator_second",
    )(neigh, lefts, field.reshape(BLK_DEV, BLOCK, RHS), recv, base, field)


def sum_kernel(regions, layers, part_ref, out_ref, hold_core, total, hold_layer, hold_chip, sems):
    region = lax.axis_index("region")
    layer = lax.axis_index("layer")
    chips = regions // 2
    core = lax.rem(region, 2)
    chip = lax.div(region, 2)
    others = (
        [(2 * chip + 1 - core, layer)]
        + [(region, lax.rem(layer + d, layers)) for d in range(1, layers)]
        + [(2 * lax.rem(chip + d, chips) + core, layer) for d in range(1, chips)]
    )
    barrier = pltpu.get_barrier_semaphore()
    for peer in others:
        pl.semaphore_signal(barrier, inc=1, device_id=peer, device_id_type=MESH)
    pl.semaphore_wait(barrier, len(others))

    def copy_of(n, source, target):
        return pltpu.make_async_remote_copy(
            src_ref=source,
            dst_ref=target,
            send_sem=sems.at[0, n],
            recv_sem=sems.at[1, n],
            device_id=others[n],
            device_id_type=MESH,
        )

    copies = [copy_of(0, part_ref, hold_core)]
    copies[0].start()
    copies[0].wait_recv()
    total[0] = part_ref[...] + hold_core[...]
    stage = [copy_of(d, total.at[0], hold_layer.at[d - 1]) for d in range(1, layers)]
    for copy in stage:
        copy.start()
    for copy in stage:
        copy.wait_recv()
    value = total[0]
    for d in range(layers - 1):
        value = value + hold_layer[d]
    total[1] = value
    copies += stage
    stage = [copy_of(layers - 1 + d, total.at[1], hold_chip.at[d - 1]) for d in range(1, chips)]
    for copy in stage:
        copy.start()
    for copy in stage:
        copy.wait_recv()
    for d in range(chips - 1):
        value = value + hold_chip[d]
    out_ref[...] = value
    copies += stage
    for copy in copies:
        copy.wait_send()


def sum_all(part, regions, layers, number):
    shape = part.shape
    chips = regions // 2
    return pl.pallas_call(
        functools.partial(sum_kernel, regions, layers),
        out_shape=jax.ShapeDtypeStruct(shape, F32),
        in_specs=[VMEM()],
        out_specs=VMEM(),
        scratch_shapes=[
            pltpu.VMEM(shape, F32),
            pltpu.VMEM((2,) + shape, F32),
            pltpu.VMEM((layers - 1,) + shape, F32),
            pltpu.VMEM((chips - 1,) + shape, F32),
            pltpu.SemaphoreType.DMA((2, layers + chips - 1)),
        ],
        compiler_params=pltpu.CompilerParams(
            collective_id=number, has_side_effects=True, vmem_limit_bytes=BIG
        ),
        name="gram_sum",
    )(part)


def eliminate(works):
    row_id = lax.broadcasted_iota(jnp.int32, (RHS, 2 * RHS), 0)
    for k in range(RHS):
        done = []
        for work in works:
            scaled = work[k : k + 1, :] * (1.0 / work[k : k + 1, k : k + 1])
            done.append(jnp.where(row_id == k, scaled, work - work[:, k : k + 1] * scaled))
        works = done
    return [work[:, RHS:] for work in works]


def solve_kernel(gram_ref, out_ref):
    norm_zero = gram_ref[0:64, 0:64]
    curve_zero = gram_ref[0:64, 64:128]
    image_gram = gram_ref[64:128, 0:64]
    base_twice = gram_ref[64:128, 64:128]
    image_twice = gram_ref[128:192, 0:64]
    eye = (
        lax.broadcasted_iota(jnp.int32, (RHS, RHS), 0)
        == lax.broadcasted_iota(jnp.int32, (RHS, RHS), 1)
    ).astype(F32)
    symmetric = 0.5 * (curve_zero + curve_zero.T)
    alpha, inverse = eliminate(
        [
            jnp.concatenate([symmetric, norm_zero], axis=1),
            jnp.concatenate([norm_zero, eye], axis=1),
        ]
    )
    crossed = dot_hi(curve_zero, alpha)
    norm_one = norm_zero - crossed - crossed.T + dot_hi(alpha, dot_hi(image_gram, alpha), ((0,), (0,)))
    blend = eye + dot_hi(inverse, norm_one)
    upper = dot_hi(curve_zero, blend) - dot_hi(base_twice, alpha)
    lower = dot_hi(image_gram, blend) - dot_hi(image_twice, alpha)
    curve_one = dot_hi(blend, upper, ((0,), (0,))) - dot_hi(alpha, lower, ((0,), (0,)))
    (alpha_second,) = eliminate(
        [jnp.concatenate([0.5 * (curve_one + curve_one.T), norm_one], axis=1)]
    )
    out_ref[0:64] = alpha + dot_hi(blend, alpha_second)
    out_ref[64:128] = -dot_hi(alpha, alpha_second)


def solve_all(gram):
    return pl.pallas_call(
        solve_kernel,
        out_shape=jax.ShapeDtypeStruct((2 * RHS, RHS), F32),
        in_specs=[VMEM()],
        out_specs=VMEM(),
        name="small_solves",
    )(gram)


def final_kernel(mix_ref, base_ref, image_ref, twice_ref, sol_ref, res_ref):
    first = mix_ref[0:64]
    second = mix_ref[64:128]
    over = ((0,), (1,))
    base = base_ref[...]
    image = image_ref[...]
    sol_ref[...] = dot_hi(first, base, ((0,), (0,))) + dot_hi(second, image, over)
    res_ref[...] = base - (dot_hi(first, image, over) + dot_hi(second, twice_ref[...], over))


def final_fields(mix, base, image, twice):
    nodes = base.shape[1]
    step = nodes // 4
    wide = pl.BlockSpec((RHS, step), lambda g: (0, g))
    tall = pl.BlockSpec((step, RHS), lambda g: (g, 0))
    return pl.pallas_call(
        final_kernel,
        grid=(nodes // step,),
        out_shape=[jax.ShapeDtypeStruct(base.shape, F32)] * 2,
        in_specs=[pl.BlockSpec((2 * RHS, RHS), lambda g: (0, 0)), wide, tall, tall],
        out_specs=[wide, wide],
        compiler_params=pltpu.CompilerParams(vmem_limit_bytes=BIG),
        name="final_fields",
    )(mix, base, image, twice)


def place_kernel(slot_ref, node_ref, base_ref, image_ref, out_ref):
    out_ref[...] = jnp.zeros_like(out_ref)

    @pl.loop(0, slot_ref.shape[0], unroll=8)
    def _(j):
        slot, node = slot_ref[j], node_ref[j]
        row = jnp.concatenate([base_ref[pl.ds(node, 1), :], image_ref[pl.ds(node, 1), :]], axis=1)
        out_ref[pl.ds(slot, 1), :] = row


def place_rows(slots, nodes, base, image, count):
    return pl.pallas_call(
        place_kernel,
        out_shape=jax.ShapeDtypeStruct((count * SLOTS, 2 * RHS), F32),
        in_specs=[SMEM(), SMEM(), VMEM(), VMEM()],
        out_specs=VMEM(),
        compiler_params=pltpu.CompilerParams(vmem_limit_bytes=BIG),
        name="place_rows",
    )(slots, nodes, base, image)


def slots_of(owners, owner_count):
    hits = (owners[:, None] == jnp.arange(owner_count, dtype=jnp.int32)[None, :]).astype(jnp.int32)
    earlier = jnp.cumsum(hits, axis=0, dtype=jnp.int32) - hits
    return owners * SLOTS + jnp.sum(earlier * hits, axis=1, dtype=jnp.int32)


def on_device(right_side, block_entries, neighbours, face_rows, die_owner, die_node):
    regions, layers = lax.axis_size("region"), lax.axis_size("layer")
    mats = block_entries.transpose(1, 0, 2)
    faces = face_rows.reshape(-1)
    neigh = neighbours.reshape(-1)
    base = right_side.T
    base_blocks = base.reshape(BLK_DEV, BLOCK, RHS)
    slots = slots_of(die_owner[:, 0], layers)
    received = exchange(faces, base_blocks, regions, layers, 0)
    image, lefts = apply_first(neigh, mats, base_blocks, received)
    received = exchange(faces, image.reshape(BLK_DEV, BLOCK, RHS), regions, layers, 0)
    twice, gram = apply_second(neigh, lefts, image, received, base)
    placed = place_rows(slots, die_node, base, image, layers)
    arrived = lax.all_to_all(
        placed.reshape(layers, SLOTS, 2 * RHS), "layer", split_axis=0, concat_axis=0, tiled=True
    )
    mix = solve_all(sum_all(gram, regions, layers, 1))
    solution_field, residual = final_fields(mix, right_side, image, twice)
    mech = jnp.dot(
        arrived.reshape(layers * SLOTS, 2 * RHS),
        mix,
        precision=lax.Precision.HIGHEST,
        preferred_element_type=F32,
    )
    return solution_field, residual, mech.reshape(layers, SLOTS * RHS)


def solution(mesh):
    in_specs = (
        P(None, ("region", "layer")),
        P(("region", "layer"), None, None),
        P(("region", "layer"), None),
        P(("region", "layer"), None),
        P(("region", "layer"), None),
        P(("region", "layer")),
    )
    out_specs = (
        P(None, ("region", "layer")),
        P(None, ("region", "layer")),
        P(("region", "layer"), None),
    )
    return jax.shard_map(
        on_device, mesh=mesh, in_specs=in_specs, out_specs=out_specs, check_vma=False
    )
```

```python
import functools

import jax
import jax.numpy as jnp
from jax import lax
from jax.experimental import pallas as pl
from jax.experimental.pallas import tpu as pltpu
from jax.sharding import PartitionSpec as P

BLOCK = 64
RHS = 64
COUPLED = 7
BLK_DEV = 64
SLOTS = 128
FACES = 8
GROUP = 8
MESH = pl.DeviceIdType.MESH
F32 = jnp.float32
BF16 = jnp.bfloat16
VMEM = functools.partial(pl.BlockSpec, memory_space=pltpu.VMEM)
SMEM = functools.partial(pl.BlockSpec, memory_space=pltpu.SMEM)
BIG = 48 * 1024 * 1024


def dot_hi(left, right, dims=((1,), (0,))):
    return lax.dot_general(
        left, right, (dims, ((), ())), precision=lax.Precision.HIGHEST, preferred_element_type=F32
    )


def exchange_kernel(regions, layers, faces_ref, field_ref, out_ref, send_buf, send_sem, recv_sem):
    region = lax.axis_index("region")
    layer = lax.axis_index("layer")
    near = region + 1 - 2 * lax.rem(region, 2)
    far = lax.rem(region + regions // 2, regions)
    peers = (
        (near, layer),
        (far, layer),
        (region, lax.max(layer - 1, 0)),
        (region, lax.min(layer + 1, layers - 1)),
    )
    has = (None, None, layer > 0, layer < layers - 1)
    landing = (0, 1, 3, 2)

    def guarded(m, action):
        if has[m] is None:
            action()
        else:
            pl.when(has[m])(action)

    barrier = pltpu.get_barrier_semaphore()
    for m in range(4):

        def greet(m=m):
            pl.semaphore_signal(barrier, inc=1, device_id=peers[m], device_id_type=MESH)

        guarded(m, greet)
    for m in range(4):
        for j in range(FACES // 2):
            first = field_ref[faces_ref[m * FACES + 2 * j]]
            second = field_ref[faces_ref[m * FACES + 2 * j + 1]]
            send_buf[m, j] = jnp.concatenate([first[:, -RHS:], second[:, -RHS:]], axis=1)
    pl.semaphore_wait(barrier, 2 + lax.min(layer, 1) + lax.min(layers - 1 - layer, 1))

    def copy_of(m):
        return pltpu.make_async_remote_copy(
            src_ref=send_buf.at[SENDS[m]],
            dst_ref=out_ref.at[landing[m]],
            send_sem=send_sem.at[m],
            recv_sem=recv_sem.at[landing[m]],
            device_id=peers[m],
            device_id_type=MESH,
        )

    for m in range(4):
        guarded(m, lambda m=m: copy_of(m).start())
    for m in (2, 3):

        def blank(m=m):
            out_ref[m] = jnp.zeros_like(out_ref[m])

        pl.when(jnp.logical_not(has[m]))(blank)
    for m in range(4):
        guarded(m, lambda m=m: copy_of(m).wait_send())
    for m in range(4):

        def arrive(m=m):
            pltpu.make_async_remote_copy(
                src_ref=send_buf.at[m],
                dst_ref=out_ref.at[m],
                send_sem=send_sem.at[m],
                recv_sem=recv_sem.at[m],
                device_id=peers[m],
                device_id_type=MESH,
            ).wait_recv()

        guarded(m, arrive)


SENDS = (0, 1, 3, 2)


def exchange(faces, field, regions, layers, number):
    return pl.pallas_call(
        functools.partial(exchange_kernel, regions, layers),
        out_shape=jax.ShapeDtypeStruct((4, FACES // 2, BLOCK, 2 * RHS), F32),
        in_specs=[SMEM(), VMEM()],
        out_specs=VMEM(),
        scratch_shapes=[
            pltpu.VMEM((4, FACES // 2, BLOCK, 2 * RHS), F32),
            pltpu.SemaphoreType.DMA((4,)),
            pltpu.SemaphoreType.DMA((4,)),
        ],
        compiler_params=pltpu.CompilerParams(
            collective_id=number, has_side_effects=True, vmem_limit_bytes=BIG
        ),
        name="face_exchange",
    )(faces, field)


def split_pair(block):
    upper = block.astype(BF16)
    return upper, (block - upper.astype(F32)).astype(BF16)


def load_extended(field_ref, recv_ref, ext):
    @pl.loop(0, BLK_DEV, unroll=4)
    def _(n):
        upper, lower = split_pair(field_ref[n][:, -RHS:])
        ext[n] = jnp.concatenate([upper, lower], axis=1)

    for m in range(4):
        for j in range(FACES // 2):
            pair = recv_ref[m, j]
            for half in range(2):
                upper, lower = split_pair(pair[:, half * RHS : (half + 1) * RHS])
                ext[BLK_DEV + m * FACES + 2 * j + half] = jnp.concatenate([upper, lower], axis=1)


def product_of(left, neigh_ref, ext, i):
    parts = [ext[i]]
    for k in range(COUPLED - 1):
        parts.append(ext[neigh_ref[i * (COUPLED - 1) + k]])
    full = jnp.dot(left, jnp.concatenate(parts, axis=0), preferred_element_type=F32)
    rows = full[:BLOCK] + full[BLOCK:]
    return rows[:, :RHS] + rows[:, RHS:]


def first_kernel(neigh_ref, mats_ref, field_ref, recv_ref, base_ref, out_ref, left_ref, ext, spread, image):
    group = pl.program_id(0)

    @pl.when(group == 0)
    def _():
        load_extended(field_ref, recv_ref, ext)

    for k in range(COUPLED):
        for c in range(BLOCK // 2):
            spread[k, pl.ds(c * GROUP, GROUP), :] = mats_ref[k, :, c * 128 : (c + 1) * 128]
    low = lax.broadcasted_iota(jnp.int32, (BLOCK // 2, 128), 1) < BLOCK
    for sub in range(GROUP):
        i = group * GROUP + sub
        tiles = [spread[k, pl.ds(sub, BLOCK // 2, stride=GROUP), :] for k in range(COUPLED)]
        turned = [pltpu.roll(tile, BLOCK, 1) for tile in tiles]
        uppers, lowers = [], []
        for k in range(0, COUPLED, 2):
            if k + 1 < COUPLED:
                even = jnp.where(low, tiles[k], turned[k + 1])
                odd = jnp.where(low, turned[k], tiles[k + 1])
            else:
                even, odd = tiles[k][:, :BLOCK], turned[k][:, :BLOCK]
            upper, lower = split_pair(jnp.concatenate([even, odd], axis=0))
            uppers.append(upper)
            lowers.append(lower)
        left = jnp.concatenate(
            [jnp.concatenate(uppers, axis=1), jnp.concatenate(lowers, axis=1)], axis=0
        )
        left_ref[sub] = left
        rows = product_of(left, neigh_ref, ext, i)
        for odd in range(2):
            image[pl.ds(sub * BLOCK + odd, BLOCK // 2, stride=2), :] = rows[
                odd * BLOCK // 2 : (odd + 1) * BLOCK // 2
            ]
    out_ref[...] = jnp.concatenate([base_ref[...], image[...]], axis=1)


def second_kernel(neigh_ref, left_ref, field_ref, recv_ref, pair_ref, out_ref, gram_ref, ext):
    group = pl.program_id(0)

    @pl.when(group == 0)
    def _():
        load_extended(field_ref, recv_ref, ext)
        gram_ref[...] = jnp.zeros_like(gram_ref)

    for sub in range(GROUP):
        i = group * GROUP + sub
        rows = product_of(left_ref[sub], neigh_ref, ext, i)
        for odd in range(2):
            out_ref[pl.ds(sub * BLOCK + odd, BLOCK // 2, stride=2), :] = rows[
                odd * BLOCK // 2 : (odd + 1) * BLOCK // 2
            ]
    pair = pair_ref[...]
    own = dot_hi(pair, pair, ((0,), (0,)))
    cross = dot_hi(pair, out_ref[...], ((0,), (0,)))
    gram_ref[0:64] += own[:64]
    gram_ref[64:128] += jnp.concatenate([own[64:, 64:], cross[:64]], axis=1)
    gram_ref[128:192] += jnp.concatenate([cross[64:], cross[64:]], axis=1)


def apply_first(neigh, mats, base, recv):
    rows = GROUP * BLOCK
    grid = BLK_DEV // GROUP
    return pl.pallas_call(
        first_kernel,
        grid=(grid,),
        out_shape=[
            jax.ShapeDtypeStruct((BLK_DEV * BLOCK, 2 * RHS), F32),
            jax.ShapeDtypeStruct((BLK_DEV, 2 * BLOCK, COUPLED * BLOCK), BF16),
        ],
        in_specs=[
            SMEM(),
            pl.BlockSpec((COUPLED, GROUP, BLOCK * BLOCK), lambda g: (0, g, 0)),
            pl.BlockSpec((BLK_DEV, BLOCK, RHS), lambda g: (0, 0, 0)),
            pl.BlockSpec((4, FACES // 2, BLOCK, 2 * RHS), lambda g: (0, 0, 0, 0)),
            pl.BlockSpec((rows, RHS), lambda g: (g, 0)),
        ],
        out_specs=[
            pl.BlockSpec((rows, 2 * RHS), lambda g: (g, 0)),
            pl.BlockSpec((GROUP, 2 * BLOCK, COUPLED * BLOCK), lambda g: (g, 0, 0)),
        ],
        scratch_shapes=[
            pltpu.VMEM((BLK_DEV + 4 * FACES, BLOCK, 2 * RHS), BF16),
            pltpu.VMEM((COUPLED, GROUP * BLOCK // 2, 128), F32),
            pltpu.VMEM((rows, RHS), F32),
        ],
        compiler_params=pltpu.CompilerParams(vmem_limit_bytes=BIG),
        name="operator_first",
    )(neigh, mats, base.reshape(BLK_DEV, BLOCK, RHS), recv, base)


def apply_second(neigh, lefts, pair, recv):
    rows = GROUP * BLOCK
    grid = BLK_DEV // GROUP
    return pl.pallas_call(
        second_kernel,
        grid=(grid,),
        out_shape=[
            jax.ShapeDtypeStruct((BLK_DEV * BLOCK, RHS), F32),
            jax.ShapeDtypeStruct((192, 128), F32),
        ],
        in_specs=[
            SMEM(),
            pl.BlockSpec((GROUP, 2 * BLOCK, COUPLED * BLOCK), lambda g: (g, 0, 0)),
            pl.BlockSpec((BLK_DEV, BLOCK, 2 * RHS), lambda g: (0, 0, 0)),
            pl.BlockSpec((4, FACES // 2, BLOCK, 2 * RHS), lambda g: (0, 0, 0, 0)),
            pl.BlockSpec((rows, 2 * RHS), lambda g: (g, 0)),
        ],
        out_specs=[
            pl.BlockSpec((rows, RHS), lambda g: (g, 0)),
            pl.BlockSpec((192, 128), lambda g: (0, 0)),
        ],
        scratch_shapes=[pltpu.VMEM((BLK_DEV + 4 * FACES, BLOCK, 2 * RHS), BF16)],
        compiler_params=pltpu.CompilerParams(vmem_limit_bytes=BIG),
        name="operator_second",
    )(neigh, lefts, pair.reshape(BLK_DEV, BLOCK, 2 * RHS), recv, pair)


def sum_kernel(regions, layers, part_ref, out_ref, hold_core, half, hold_layer, piece, hold_chip, sems):
    region = lax.axis_index("region")
    layer = lax.axis_index("layer")
    chips = regions // 2
    core = lax.rem(region, 2)
    chip = lax.div(region, 2)
    mate = (2 * chip + 1 - core, layer)
    across = [(region, lax.rem(layer + d, layers)) for d in range(1, layers)]
    along = [(2 * lax.rem(chip + d, chips) + core, layer) for d in range(1, chips)]
    rows = part_ref.shape[0]
    half_rows = rows // 2
    share = half_rows // layers
    barrier = pltpu.get_barrier_semaphore()
    for peer in [mate] + across + along:
        pl.semaphore_signal(barrier, inc=1, device_id=peer, device_id_type=MESH)
    pl.semaphore_wait(barrier, layers + chips - 1)
    used = []

    def send(source, target, peer):
        n = len(used)
        copy = pltpu.make_async_remote_copy(
            src_ref=source,
            dst_ref=target,
            send_sem=sems.at[0, n],
            recv_sem=sems.at[1, n],
            device_id=peer,
            device_id_type=MESH,
        )
        used.append(copy)
        copy.start()
        return copy

    def half_of(which):
        return pl.ds(pl.multiple_of(which * half_rows, 8), half_rows)

    def share_of(which):
        return pl.ds(pl.multiple_of(which * share, 8), share)

    def in_out(which):
        return pl.ds(pl.multiple_of(core * half_rows + which * share, 8), share)

    send(part_ref.at[half_of(1 - core)], hold_core, mate).wait_recv()
    half[...] = part_ref[half_of(core)] + hold_core[...]
    stage = [
        send(half.at[share_of(lax.rem(layer + d, layers))], hold_layer.at[d - 1], across[d - 1])
        for d in range(1, layers)
    ]
    for copy in stage:
        copy.wait_recv()
    value = half[share_of(layer)]
    for d in range(layers - 1):
        value = value + hold_layer[d]
    piece[...] = value
    stage = [send(piece, hold_chip.at[d - 1], along[d - 1]) for d in range(1, chips)]
    for copy in stage:
        copy.wait_recv()
    for d in range(chips - 1):
        value = value + hold_chip[d]
    mine = in_out(layer)
    out_ref[mine] = value
    stage = [send(out_ref.at[mine], out_ref.at[mine], peer) for peer in across]
    for copy in stage:
        copy.wait_recv()
    own = half_of(core)
    send(out_ref.at[own], out_ref.at[own], mate).wait_recv()
    for copy in used:
        copy.wait_send()


def sum_all(part, regions, layers, number):
    rows, lanes = part.shape
    chips = regions // 2
    share = rows // 2 // layers
    return pl.pallas_call(
        functools.partial(sum_kernel, regions, layers),
        out_shape=jax.ShapeDtypeStruct(part.shape, F32),
        in_specs=[VMEM()],
        out_specs=VMEM(),
        scratch_shapes=[
            pltpu.VMEM((rows // 2, lanes), F32),
            pltpu.VMEM((rows // 2, lanes), F32),
            pltpu.VMEM((layers - 1, share, lanes), F32),
            pltpu.VMEM((share, lanes), F32),
            pltpu.VMEM((chips - 1, share, lanes), F32),
            pltpu.SemaphoreType.DMA((2, 2 * layers + chips - 1)),
        ],
        compiler_params=pltpu.CompilerParams(
            collective_id=number, has_side_effects=True, vmem_limit_bytes=BIG
        ),
        name="gram_sum",
    )(part)


PIVOTS = 4


def eliminate_block(work, k, row_id):
    columns = [
        jnp.broadcast_to(work[:, k + j : k + j + 1], work.shape) for j in range(PIVOTS)
    ]
    rows = [work[k + i : k + i + 1, :] for i in range(PIVOTS)]
    small = [[columns[j][k + i : k + i + 1, :] for j in range(PIVOTS)] for i in range(PIVOTS)]
    for i in range(PIVOTS):
        inverse = 1.0 / small[i][i]
        rows[i] = rows[i] * inverse
        small[i] = [value * inverse for value in small[i]]
        for j in range(PIVOTS):
            if j != i:
                factor = small[j][i]
                rows[j] = rows[j] - factor * rows[i]
                small[j] = [
                    small[j][c] - factor * small[i][c] if c > i else small[j][c]
                    for c in range(PIVOTS)
                ]
    result = work
    for j in range(PIVOTS):
        result = result - columns[j] * rows[j]
    for j in range(PIVOTS):
        result = jnp.where(row_id == k + j, rows[j], result)
    return result


def eliminate(works):
    row_id = lax.broadcasted_iota(jnp.int32, (RHS, 2 * RHS), 0)
    for k in range(0, RHS, PIVOTS):
        works = [eliminate_block(work, k, row_id) for work in works]
    return [work[:, RHS:] for work in works]


def solve_kernel(gram_ref, out_ref):
    norm_zero = gram_ref[0:64, 0:64]
    curve_zero = gram_ref[0:64, 64:128]
    image_gram = gram_ref[64:128, 0:64]
    base_twice = gram_ref[64:128, 64:128]
    image_twice = gram_ref[128:192, 0:64]
    eye = (
        lax.broadcasted_iota(jnp.int32, (RHS, RHS), 0)
        == lax.broadcasted_iota(jnp.int32, (RHS, RHS), 1)
    ).astype(F32)
    symmetric = 0.5 * (curve_zero + curve_zero.T)
    alpha, inverse = eliminate(
        [
            jnp.concatenate([symmetric, norm_zero], axis=1),
            jnp.concatenate([norm_zero, eye], axis=1),
        ]
    )
    crossed = dot_hi(curve_zero, alpha)
    norm_one = norm_zero - crossed - crossed.T + dot_hi(alpha, dot_hi(image_gram, alpha), ((0,), (0,)))
    blend = eye + dot_hi(inverse, norm_one)
    upper = dot_hi(curve_zero, blend) - dot_hi(base_twice, alpha)
    lower = dot_hi(image_gram, blend) - dot_hi(image_twice, alpha)
    curve_one = dot_hi(blend, upper, ((0,), (0,))) - dot_hi(alpha, lower, ((0,), (0,)))
    (alpha_second,) = eliminate(
        [jnp.concatenate([0.5 * (curve_one + curve_one.T), norm_one], axis=1)]
    )
    first = alpha + dot_hi(blend, alpha_second)
    second = -dot_hi(alpha, alpha_second)
    blank = jnp.zeros_like(first)
    out_ref[0:64] = jnp.concatenate([first, blank], axis=1)
    out_ref[64:128] = jnp.concatenate([second, first], axis=1)
    out_ref[128:192] = jnp.concatenate([blank, second], axis=1)


def solve_all(gram):
    return pl.pallas_call(
        solve_kernel,
        out_shape=jax.ShapeDtypeStruct((3 * RHS, 2 * RHS), F32),
        in_specs=[VMEM()],
        out_specs=VMEM(),
        name="small_solves",
    )(gram)


def final_kernel(mix_ref, base_ref, pair_ref, twice_ref, sol_ref, res_ref):
    both = dot_hi(pair_ref[...], mix_ref[0:128]) + dot_hi(twice_ref[...], mix_ref[128:192])
    turned = both.T
    sol_ref[...] = turned[:RHS]
    res_ref[...] = base_ref[...] - turned[RHS:]


def final_fields(mix, base, pair, twice):
    nodes = base.shape[1]
    step = nodes // 4
    wide = pl.BlockSpec((RHS, step), lambda g: (0, g))
    return pl.pallas_call(
        final_kernel,
        grid=(nodes // step,),
        out_shape=[jax.ShapeDtypeStruct(base.shape, F32)] * 2,
        in_specs=[
            pl.BlockSpec((3 * RHS, 2 * RHS), lambda g: (0, 0)),
            wide,
            pl.BlockSpec((step, 2 * RHS), lambda g: (g, 0)),
            pl.BlockSpec((step, RHS), lambda g: (g, 0)),
        ],
        out_specs=[wide, wide],
        compiler_params=pltpu.CompilerParams(vmem_limit_bytes=BIG),
        name="final_fields",
    )(mix, base, pair, twice)


def place_kernel(slot_ref, node_ref, pair_ref, out_ref):
    out_ref[...] = jnp.zeros_like(out_ref)

    @pl.loop(0, slot_ref.shape[0], step=16)
    def _(start):
        rows = [pair_ref[pl.ds(node_ref[start + j], 1), :] for j in range(16)]
        for j in range(16):
            out_ref[pl.ds(slot_ref[start + j], 1), :] = rows[j]


def place_rows(slots, nodes, pair, count):
    return pl.pallas_call(
        place_kernel,
        out_shape=jax.ShapeDtypeStruct((count * SLOTS, 2 * RHS), F32),
        in_specs=[SMEM(), SMEM(), VMEM()],
        out_specs=VMEM(),
        compiler_params=pltpu.CompilerParams(vmem_limit_bytes=BIG),
        name="place_rows",
    )(slots, nodes, pair)


def slots_of(owners, owner_count):
    hits = (owners[:, None] == jnp.arange(owner_count, dtype=jnp.int32)[None, :]).astype(jnp.int32)
    earlier = jnp.cumsum(hits, axis=0, dtype=jnp.int32) - hits
    return owners * SLOTS + jnp.sum(earlier * hits, axis=1, dtype=jnp.int32)


def on_device(right_side, block_entries, neighbours, face_rows, die_owner, die_node):
    regions, layers = lax.axis_size("region"), lax.axis_size("layer")
    mats = block_entries.transpose(1, 0, 2)
    faces = face_rows.reshape(-1)
    neigh = neighbours.reshape(-1)
    base = right_side.T
    base_blocks = base.reshape(BLK_DEV, BLOCK, RHS)
    slots = slots_of(die_owner[:, 0], layers)
    received = exchange(faces, base_blocks, regions, layers, 0)
    pair, lefts = apply_first(neigh, mats, base, received)
    received = exchange(faces, pair.reshape(BLK_DEV, BLOCK, 2 * RHS), regions, layers, 2)
    twice, gram = apply_second(neigh, lefts, pair, received)
    gram = jnp.pad(gram, ((0, -gram.shape[0] % (16 * layers)), (0, 0)))
    placed = place_rows(slots, die_node, pair, layers)
    arrived = lax.all_to_all(
        placed.reshape(layers, SLOTS, 2 * RHS), "layer", split_axis=0, concat_axis=0, tiled=True
    )
    mix = solve_all(sum_all(gram, regions, layers, 1))
    solution_field, residual = final_fields(mix, right_side, pair, twice)
    mech = jnp.dot(
        arrived.reshape(layers * SLOTS, 2 * RHS),
        mix[: 2 * RHS, :RHS],
        precision=lax.Precision.HIGHEST,
        preferred_element_type=F32,
    )
    return solution_field, residual, mech.reshape(layers, SLOTS * RHS)


def solution(mesh):
    in_specs = (
        P(None, ("region", "layer")),
        P(("region", "layer"), None, None),
        P(("region", "layer"), None),
        P(("region", "layer"), None),
        P(("region", "layer"), None),
        P(("region", "layer")),
    )
    out_specs = (
        P(None, ("region", "layer")),
        P(None, ("region", "layer")),
        P(("region", "layer"), None),
    )
    return jax.shard_map(
        on_device, mesh=mesh, in_specs=in_specs, out_specs=out_specs, check_vma=False
    )
```

```python
import functools

import jax
import jax.numpy as jnp
from jax import lax
from jax.experimental import pallas as pl
from jax.experimental.pallas import tpu as pltpu
from jax.sharding import PartitionSpec as P

BLOCK = 64
RHS = 64
COUPLED = 7
BLK_DEV = 64
SLOTS = 128
FACES = 8
GROUP = 8
MESH = pl.DeviceIdType.MESH
F32 = jnp.float32
BF16 = jnp.bfloat16
VMEM = functools.partial(pl.BlockSpec, memory_space=pltpu.VMEM)
SMEM = functools.partial(pl.BlockSpec, memory_space=pltpu.SMEM)
BIG = 20 * 1024 * 1024
WIDE = 56 * 1024 * 1024


def dot_hi(left, right, dims=((1,), (0,))):
    return lax.dot_general(
        left, right, (dims, ((), ())), precision=lax.Precision.HIGHEST, preferred_element_type=F32
    )


def exchange_kernel(regions, layers, faces_ref, field_ref, out_ref, send_buf, send_sem, recv_sem):
    region = lax.axis_index("region")
    layer = lax.axis_index("layer")
    near = region + 1 - 2 * lax.rem(region, 2)
    far = lax.rem(region + regions // 2, regions)
    peers = (
        (near, layer),
        (far, layer),
        (region, lax.max(layer - 1, 0)),
        (region, lax.min(layer + 1, layers - 1)),
    )
    has = (None, None, layer > 0, layer < layers - 1)
    landing = (0, 1, 3, 2)

    def guarded(m, action):
        if has[m] is None:
            action()
        else:
            pl.when(has[m])(action)

    barrier = pltpu.get_barrier_semaphore()
    for m in range(4):

        def greet(m=m):
            pl.semaphore_signal(barrier, inc=1, device_id=peers[m], device_id_type=MESH)

        guarded(m, greet)
    for m in range(4):
        for j in range(FACES // 2):
            first = field_ref[faces_ref[m * FACES + 2 * j]]
            second = field_ref[faces_ref[m * FACES + 2 * j + 1]]
            send_buf[m, j] = jnp.concatenate([first[:, -RHS:], second[:, -RHS:]], axis=1)
    pl.semaphore_wait(barrier, 2 + lax.min(layer, 1) + lax.min(layers - 1 - layer, 1))

    def copy_of(m):
        return pltpu.make_async_remote_copy(
            src_ref=send_buf.at[SENDS[m]],
            dst_ref=out_ref.at[landing[m]],
            send_sem=send_sem.at[m],
            recv_sem=recv_sem.at[landing[m]],
            device_id=peers[m],
            device_id_type=MESH,
        )

    for m in range(4):
        guarded(m, lambda m=m: copy_of(m).start())
    for m in (2, 3):

        def blank(m=m):
            out_ref[m] = jnp.zeros_like(out_ref[m])

        pl.when(jnp.logical_not(has[m]))(blank)
    for m in range(4):
        guarded(m, lambda m=m: copy_of(m).wait_send())
    for m in range(4):

        def arrive(m=m):
            pltpu.make_async_remote_copy(
                src_ref=send_buf.at[m],
                dst_ref=out_ref.at[m],
                send_sem=send_sem.at[m],
                recv_sem=recv_sem.at[m],
                device_id=peers[m],
                device_id_type=MESH,
            ).wait_recv()

        guarded(m, arrive)


SENDS = (0, 1, 3, 2)


def exchange(faces, field, regions, layers, number):
    return pl.pallas_call(
        functools.partial(exchange_kernel, regions, layers),
        out_shape=jax.ShapeDtypeStruct((4, FACES // 2, BLOCK, 2 * RHS), F32),
        in_specs=[SMEM(), VMEM()],
        out_specs=VMEM(),
        scratch_shapes=[
            pltpu.VMEM((4, FACES // 2, BLOCK, 2 * RHS), F32),
            pltpu.SemaphoreType.DMA((4,)),
            pltpu.SemaphoreType.DMA((4,)),
        ],
        compiler_params=pltpu.CompilerParams(
            collective_id=number, has_side_effects=True, vmem_limit_bytes=BIG
        ),
        cost_estimate=pl.CostEstimate(flops=0, bytes_accessed=30_000_000, transcendentals=0),
        name="face_exchange",
    )(faces, field)


def split_pair(block):
    upper = block.astype(BF16)
    return upper, (block - upper.astype(F32)).astype(BF16)


def load_extended(field_ref, recv_ref, ext):
    @pl.loop(0, BLK_DEV, unroll=4)
    def _(n):
        upper, lower = split_pair(field_ref[n][:, -RHS:])
        ext[n] = jnp.concatenate([upper, lower], axis=1)

    for m in range(4):
        for j in range(FACES // 2):
            pair = recv_ref[m, j]
            for half in range(2):
                upper, lower = split_pair(pair[:, half * RHS : (half + 1) * RHS])
                ext[BLK_DEV + m * FACES + 2 * j + half] = jnp.concatenate([upper, lower], axis=1)


def product_of(left, neigh_ref, ext, i):
    parts = [ext[i]]
    for k in range(COUPLED - 1):
        parts.append(ext[neigh_ref[i * (COUPLED - 1) + k]])
    full = jnp.dot(left, jnp.concatenate(parts, axis=0), preferred_element_type=F32)
    rows = full[:BLOCK] + full[BLOCK:]
    return rows[:, :RHS] + rows[:, RHS:]


def first_kernel(neigh_ref, mats_ref, field_ref, recv_ref, base_ref, out_ref, left_ref, ext, spread, image):
    group = pl.program_id(0)

    @pl.when(group == 0)
    def _():
        load_extended(field_ref, recv_ref, ext)

    for k in range(COUPLED):
        for c in range(BLOCK // 2):
            spread[k, pl.ds(c * GROUP, GROUP), :] = mats_ref[k, :, c * 128 : (c + 1) * 128]
    low = lax.broadcasted_iota(jnp.int32, (BLOCK // 2, 128), 1) < BLOCK
    for sub in range(GROUP):
        i = group * GROUP + sub
        tiles = [spread[k, pl.ds(sub, BLOCK // 2, stride=GROUP), :] for k in range(COUPLED)]
        turned = [pltpu.roll(tile, BLOCK, 1) for tile in tiles]
        uppers, lowers = [], []
        for k in range(0, COUPLED, 2):
            if k + 1 < COUPLED:
                even = jnp.where(low, tiles[k], turned[k + 1])
                odd = jnp.where(low, turned[k], tiles[k + 1])
            else:
                even, odd = tiles[k][:, :BLOCK], turned[k][:, :BLOCK]
            upper, lower = split_pair(jnp.concatenate([even, odd], axis=0))
            uppers.append(upper)
            lowers.append(lower)
        left = jnp.concatenate(
            [jnp.concatenate(uppers, axis=1), jnp.concatenate(lowers, axis=1)], axis=0
        )
        left_ref[sub] = left
        rows = product_of(left, neigh_ref, ext, i)
        for odd in range(2):
            image[pl.ds(sub * BLOCK + odd, BLOCK // 2, stride=2), :] = rows[
                odd * BLOCK // 2 : (odd + 1) * BLOCK // 2
            ]
    out_ref[...] = jnp.concatenate([base_ref[...], image[...]], axis=1)


def second_kernel(neigh_ref, left_ref, field_ref, recv_ref, pair_ref, out_ref, gram_ref, ext):
    group = pl.program_id(0)

    @pl.when(group == 0)
    def _():
        load_extended(field_ref, recv_ref, ext)
        gram_ref[...] = jnp.zeros_like(gram_ref)

    for sub in range(GROUP):
        i = group * GROUP + sub
        rows = product_of(left_ref[sub], neigh_ref, ext, i)
        for odd in range(2):
            out_ref[pl.ds(sub * BLOCK + odd, BLOCK // 2, stride=2), :] = rows[
                odd * BLOCK // 2 : (odd + 1) * BLOCK // 2
            ]
    left = jnp.concatenate(split_pair(pair_ref[...]), axis=1)
    right = jnp.concatenate(split_pair(out_ref[...]), axis=1)
    over = (((0,), (0,)), ((), ()))
    own = lax.dot_general(left, left, over, preferred_element_type=F32)
    cross = lax.dot_general(left, right, over, preferred_element_type=F32)
    own = own[:128] + own[128:]
    own = own[:, :128] + own[:, 128:]
    cross = cross[:128] + cross[128:]
    cross = cross[:, :RHS] + cross[:, RHS:]
    gram_ref[0:64] += own[:64]
    gram_ref[64:128] += jnp.concatenate([own[64:, 64:], cross[:64]], axis=1)
    gram_ref[128:192] += jnp.concatenate([cross[64:], cross[64:]], axis=1)


def apply_first(neigh, mats, base, recv):
    rows = GROUP * BLOCK
    grid = BLK_DEV // GROUP
    return pl.pallas_call(
        first_kernel,
        grid=(grid,),
        out_shape=[
            jax.ShapeDtypeStruct((BLK_DEV * BLOCK, 2 * RHS), F32),
            jax.ShapeDtypeStruct((BLK_DEV, 2 * BLOCK, COUPLED * BLOCK), BF16),
        ],
        in_specs=[
            SMEM(),
            pl.BlockSpec((COUPLED, GROUP, BLOCK * BLOCK), lambda g: (0, g, 0)),
            pl.BlockSpec((BLK_DEV, BLOCK, RHS), lambda g: (0, 0, 0)),
            pl.BlockSpec((4, FACES // 2, BLOCK, 2 * RHS), lambda g: (0, 0, 0, 0)),
            pl.BlockSpec((rows, RHS), lambda g: (g, 0)),
        ],
        out_specs=[
            pl.BlockSpec((rows, 2 * RHS), lambda g: (g, 0)),
            pl.BlockSpec((GROUP, 2 * BLOCK, COUPLED * BLOCK), lambda g: (g, 0, 0)),
        ],
        scratch_shapes=[
            pltpu.VMEM((BLK_DEV + 4 * FACES, BLOCK, 2 * RHS), BF16),
            pltpu.VMEM((COUPLED, GROUP * BLOCK // 2, 128), F32),
            pltpu.VMEM((rows, RHS), F32),
        ],
        compiler_params=pltpu.CompilerParams(vmem_limit_bytes=WIDE),
        name="operator_first",
    )(neigh, mats, base.reshape(BLK_DEV, BLOCK, RHS), recv, base)


def apply_second(neigh, lefts, pair, recv):
    rows = GROUP * BLOCK
    grid = BLK_DEV // GROUP
    return pl.pallas_call(
        second_kernel,
        grid=(grid,),
        out_shape=[
            jax.ShapeDtypeStruct((BLK_DEV * BLOCK, RHS), F32),
            jax.ShapeDtypeStruct((192, 128), F32),
        ],
        in_specs=[
            SMEM(),
            pl.BlockSpec((GROUP, 2 * BLOCK, COUPLED * BLOCK), lambda g: (g, 0, 0)),
            pl.BlockSpec((BLK_DEV, BLOCK, 2 * RHS), lambda g: (0, 0, 0)),
            pl.BlockSpec((4, FACES // 2, BLOCK, 2 * RHS), lambda g: (0, 0, 0, 0)),
            pl.BlockSpec((rows, 2 * RHS), lambda g: (g, 0)),
        ],
        out_specs=[
            pl.BlockSpec((rows, RHS), lambda g: (g, 0)),
            pl.BlockSpec((192, 128), lambda g: (0, 0)),
        ],
        scratch_shapes=[pltpu.VMEM((BLK_DEV + 4 * FACES, BLOCK, 2 * RHS), BF16)],
        compiler_params=pltpu.CompilerParams(vmem_limit_bytes=BIG),
        name="operator_second",
    )(neigh, lefts, pair.reshape(BLK_DEV, BLOCK, 2 * RHS), recv, pair)


def sum_kernel(regions, layers, part_ref, rows_ref, out_ref, moved_ref, hold_plane, piece, hold_chip, sems):
    region = lax.axis_index("region")
    layer = lax.axis_index("layer")
    chips = regions // 2
    core = lax.rem(region, 2)
    chip = lax.div(region, 2)
    members = 2 * layers
    plane = [
        (2 * chip + lax.rem(core + b, 2), lax.rem(layer + d, layers))
        for b in range(2)
        for d in range(layers)
    ][1:]
    along = [(2 * lax.rem(chip + d, chips) + core, layer) for d in range(1, chips)]
    share = part_ref.shape[0] // members
    barrier = pltpu.get_barrier_semaphore()
    for peer in plane + along:
        pl.semaphore_signal(barrier, inc=1, device_id=peer, device_id_type=MESH)
    pl.semaphore_wait(barrier, members + chips - 2)
    used = []

    def send(source, target, peer):
        n = len(used)
        copy = pltpu.make_async_remote_copy(
            src_ref=source,
            dst_ref=target,
            send_sem=sems.at[0, n],
            recv_sem=sems.at[1, n],
            device_id=peer,
            device_id_type=MESH,
        )
        used.append(copy)
        copy.start()
        return copy

    def share_of(place):
        which = lax.rem(place[0], 2) * layers + place[1]
        return pl.ds(pl.multiple_of(which * share, 8), share)

    mine = share_of((region, layer))
    stage = [send(part_ref.at[share_of(peer)], hold_plane.at[n], peer) for n, peer in enumerate(plane)]
    rows_moving = [
        send(rows_ref.at[peer[1]], moved_ref.at[layer], peer) for peer in plane[: layers - 1]
    ]
    moved_ref[layer] = rows_ref[layer]
    for copy in stage:
        copy.wait_recv()
    value = part_ref[mine]
    for n in range(members - 1):
        value = value + hold_plane[n]
    piece[...] = value
    stage = [send(piece, hold_chip.at[d], peer) for d, peer in enumerate(along)]
    for copy in stage:
        copy.wait_recv()
    for d in range(chips - 1):
        value = value + hold_chip[d]
    out_ref[mine] = value
    stage = [send(out_ref.at[mine], out_ref.at[mine], peer) for peer in plane]
    for copy in stage + rows_moving:
        copy.wait_recv()
    for copy in used:
        copy.wait_send()


def sum_all(part, rows, regions, layers, number):
    lanes = part.shape[1]
    chips = regions // 2
    members = 2 * layers
    share = part.shape[0] // members
    copies = 2 * (members - 1) + (layers - 1) + (chips - 1)
    return pl.pallas_call(
        functools.partial(sum_kernel, regions, layers),
        out_shape=[
            jax.ShapeDtypeStruct(part.shape, F32),
            jax.ShapeDtypeStruct(rows.shape, F32),
        ],
        in_specs=[VMEM(), VMEM()],
        out_specs=[VMEM(), VMEM()],
        scratch_shapes=[
            pltpu.VMEM((members - 1, share, lanes), F32),
            pltpu.VMEM((share, lanes), F32),
            pltpu.VMEM((chips - 1, share, lanes), F32),
            pltpu.SemaphoreType.DMA((2, copies)),
        ],
        compiler_params=pltpu.CompilerParams(
            collective_id=number, has_side_effects=True, vmem_limit_bytes=BIG
        ),
        name="gram_sum",
    )(part, rows)


PIVOTS = 4


def eliminate_block(work, k, row_id):
    columns = [
        jnp.broadcast_to(work[:, k + j : k + j + 1], work.shape) for j in range(PIVOTS)
    ]
    rows = [work[k + i : k + i + 1, :] for i in range(PIVOTS)]
    small = [[columns[j][k + i : k + i + 1, :] for j in range(PIVOTS)] for i in range(PIVOTS)]
    for i in range(PIVOTS):
        inverse = 1.0 / small[i][i]
        rows[i] = rows[i] * inverse
        small[i] = [value * inverse for value in small[i]]
        for j in range(PIVOTS):
            if j != i:
                factor = small[j][i]
                rows[j] = rows[j] - factor * rows[i]
                small[j] = [
                    small[j][c] - factor * small[i][c] if c > i else small[j][c]
                    for c in range(PIVOTS)
                ]
    result = work
    for j in range(PIVOTS):
        result = result - columns[j] * rows[j]
    for j in range(PIVOTS):
        result = jnp.where(row_id == k + j, rows[j], result)
    return result


def eliminate(works):
    row_id = lax.broadcasted_iota(jnp.int32, (RHS, 2 * RHS), 0)
    for k in range(0, RHS, PIVOTS):
        works = [eliminate_block(work, k, row_id) for work in works]
    return [work[:, RHS:] for work in works]


def solve_kernel(gram_ref, out_ref):
    norm_zero = gram_ref[0:64, 0:64]
    curve_zero = gram_ref[0:64, 64:128]
    image_gram = gram_ref[64:128, 0:64]
    base_twice = gram_ref[64:128, 64:128]
    image_twice = gram_ref[128:192, 0:64]
    eye = (
        lax.broadcasted_iota(jnp.int32, (RHS, RHS), 0)
        == lax.broadcasted_iota(jnp.int32, (RHS, RHS), 1)
    ).astype(F32)
    symmetric = 0.5 * (curve_zero + curve_zero.T)
    alpha, inverse = eliminate(
        [
            jnp.concatenate([symmetric, norm_zero], axis=1),
            jnp.concatenate([norm_zero, eye], axis=1),
        ]
    )
    crossed = dot_hi(curve_zero, alpha)
    norm_one = norm_zero - crossed - crossed.T + dot_hi(alpha, dot_hi(image_gram, alpha), ((0,), (0,)))
    blend = eye + dot_hi(inverse, norm_one)
    upper = dot_hi(curve_zero, blend) - dot_hi(base_twice, alpha)
    lower = dot_hi(image_gram, blend) - dot_hi(image_twice, alpha)
    curve_one = dot_hi(blend, upper, ((0,), (0,))) - dot_hi(alpha, lower, ((0,), (0,)))
    (alpha_second,) = eliminate(
        [jnp.concatenate([0.5 * (curve_one + curve_one.T), norm_one], axis=1)]
    )
    first = alpha + dot_hi(blend, alpha_second)
    second = -dot_hi(alpha, alpha_second)
    blank = jnp.zeros_like(first)
    out_ref[0:64] = jnp.concatenate([first, blank], axis=1)
    out_ref[64:128] = jnp.concatenate([second, first], axis=1)
    out_ref[128:192] = jnp.concatenate([blank, second], axis=1)


def solve_all(gram):
    return pl.pallas_call(
        solve_kernel,
        out_shape=jax.ShapeDtypeStruct((3 * RHS, 2 * RHS), F32),
        in_specs=[VMEM()],
        out_specs=VMEM(),
        name="small_solves",
    )(gram)


def final_kernel(mix_ref, base_ref, pair_ref, twice_ref, sol_ref, res_ref):
    both = dot_hi(pair_ref[...], mix_ref[0:128]) + dot_hi(twice_ref[...], mix_ref[128:192])
    turned = both.T
    sol_ref[...] = turned[:RHS]
    res_ref[...] = base_ref[...] - turned[RHS:]


def final_fields(mix, base, pair, twice):
    nodes = base.shape[1]
    step = nodes // 4
    wide = pl.BlockSpec((RHS, step), lambda g: (0, g))
    return pl.pallas_call(
        final_kernel,
        grid=(nodes // step,),
        out_shape=[jax.ShapeDtypeStruct(base.shape, F32)] * 2,
        in_specs=[
            pl.BlockSpec((3 * RHS, 2 * RHS), lambda g: (0, 0)),
            wide,
            pl.BlockSpec((step, 2 * RHS), lambda g: (g, 0)),
            pl.BlockSpec((step, RHS), lambda g: (g, 0)),
        ],
        out_specs=[wide, wide],
        compiler_params=pltpu.CompilerParams(vmem_limit_bytes=BIG),
        name="final_fields",
    )(mix, base, pair, twice)


def place_kernel(slot_ref, node_ref, pair_ref, out_ref):
    out_ref[...] = jnp.zeros_like(out_ref)

    @pl.loop(0, slot_ref.shape[0], step=16)
    def _(start):
        rows = [pair_ref[pl.ds(node_ref[start + j], 1), :] for j in range(16)]
        for j in range(16):
            out_ref[pl.ds(slot_ref[start + j], 1), :] = rows[j]


def place_rows(slots, nodes, pair, count):
    return pl.pallas_call(
        place_kernel,
        out_shape=jax.ShapeDtypeStruct((count * SLOTS, 2 * RHS), F32),
        in_specs=[SMEM(), SMEM(), VMEM()],
        out_specs=VMEM(),
        compiler_params=pltpu.CompilerParams(vmem_limit_bytes=BIG),
        name="place_rows",
    )(slots, nodes, pair)


def slots_of(owners, owner_count):
    hits = (owners[:, None] == jnp.arange(owner_count, dtype=jnp.int32)[None, :]).astype(jnp.int32)
    earlier = jnp.cumsum(hits, axis=0, dtype=jnp.int32) - hits
    return owners * SLOTS + jnp.sum(earlier * hits, axis=1, dtype=jnp.int32)


def on_device(right_side, block_entries, neighbours, face_rows, die_owner, die_node):
    regions, layers = lax.axis_size("region"), lax.axis_size("layer")
    mats = block_entries.transpose(1, 0, 2)
    faces = face_rows.reshape(-1)
    neigh = neighbours.reshape(-1)
    base = right_side.T
    base_blocks = base.reshape(BLK_DEV, BLOCK, RHS)
    slots = slots_of(die_owner[:, 0], layers)
    received = exchange(faces, base_blocks, regions, layers, 0)
    pair, lefts = apply_first(neigh, mats, base, received)
    received = exchange(faces, pair.reshape(BLK_DEV, BLOCK, 2 * RHS), regions, layers, 2)
    twice, gram = apply_second(neigh, lefts, pair, received)
    gram = jnp.pad(gram, ((0, -gram.shape[0] % (16 * layers)), (0, 0)))
    placed = place_rows(slots, die_node, pair, layers)
    gram, arrived = sum_all(gram, placed.reshape(layers, SLOTS, 2 * RHS), regions, layers, 1)
    mix = solve_all(gram)
    solution_field, residual = final_fields(mix, right_side, pair, twice)
    mech = jnp.dot(
        arrived.reshape(layers * SLOTS, 2 * RHS),
        mix[: 2 * RHS, :RHS],
        precision=lax.Precision.HIGHEST,
        preferred_element_type=F32,
    )
    return solution_field, residual, mech.reshape(layers, SLOTS * RHS)


def solution(mesh):
    in_specs = (
        P(None, ("region", "layer")),
        P(("region", "layer"), None, None),
        P(("region", "layer"), None),
        P(("region", "layer"), None),
        P(("region", "layer"), None),
        P(("region", "layer")),
    )
    out_specs = (
        P(None, ("region", "layer")),
        P(None, ("region", "layer")),
        P(("region", "layer"), None),
    )
    return jax.shard_map(
        on_device, mesh=mesh, in_specs=in_specs, out_specs=out_specs, check_vma=False
    )
```
